32 devices in a mesh: ctx: 8 (over z, y), tp: 4 (over x, core).
Axes of the slice: x: 2, y: 2, z: 4, core: 2. Of those that a mesh axis runs over, the one named last changes fastest.
Arguments:
- tokens: bfloat16 [4096, 4096], P('ctx', 'tp'), may hold values from -6 to 6
- qkv_blocks: bfloat16 [3, 4, 1024, 1024], P(None, None, None, 'tp'), may hold values from -0.046875 to 0.046875
- out_blocks: bfloat16 [4, 1024, 1024], P(None, 'tp'), may hold values from -0.046875 to 0.046875
- mix_factors: float32 [4, 4, 4, 4], replicated, may hold values from -4 to 4
- head_gain: float32 [4, 1024], P(None, 'tp'), may hold values from 0.1 to 1.9
Outputs:
- layer_out: bfloat16 [4096, 4096], P('ctx', 'tp')
The draws below stay inside these ranges and needn't reach their ends.
All inputs are finite; a program needn't handle non-finite values.
Results may differ from the reference program's by a relative error of at most 0.025.
Values may be sent and summed in bfloat16 or wider, within the bound.
A program may use at most 128 MiB of HBM per device.

```python
import jax
import jax.numpy as jnp
from jax import lax

D = 4096
HEADS = 32
PHM = 4
SPAN = 128
HEAD = 128
BLOCK = 1024
SEQ = 4096
N_TP = 4


def shard_levels(own_key, dims, split, low, high):
    def one(position, shards_of):
        draws = jax.random.uniform(jax.random.fold_in(jax.random.fold_in(own_key, 6), position), (shards_of,), jnp.float32, low / len(split), high / len(split))
        return jnp.repeat(jnp.exp(draws), dims[position] // shards_of).reshape((-1,) + (1,) * (len(dims) - position - 1))

    loudness = one(*split[0])
    for cut in split[1:]:
        loudness = loudness * one(*cut)
    return loudness


def gaussian(rng, dims, width, limit, cuts=(), dtype=jnp.bfloat16):
    entries = width * jax.random.normal(rng, dims, jnp.float32)
    if cuts:
        entries = entries * shard_levels(rng, dims, cuts, -0.22, 0.18)
    return jnp.clip(entries, -limit, limit).astype(dtype)


def setup_inputs(seed: int = 0) -> dict:
    arg_keys = jax.random.split(jax.random.key(seed), 6)
    return {
        "tokens": gaussian(arg_keys[0], (SEQ, D), 1.0, 6.0, ((0, 8), (1, 4))),
        "qkv_blocks": gaussian(arg_keys[1], (3, PHM, BLOCK, BLOCK), (4 * D) ** -0.5, 0.046875, ((3, 4),)),
        "out_blocks": gaussian(arg_keys[2], (PHM, BLOCK, BLOCK), (4 * D) ** -0.5, 0.046875, ((1, 4),)),
        "mix_factors": gaussian(arg_keys[3], (4, PHM, PHM, PHM), 1.0, 4.0, (), jnp.float32),
        "head_gain": jnp.clip(1.0 + 0.18 * jax.random.normal(arg_keys[4], (PHM, BLOCK), jnp.float32), 0.1, 1.9),
    }


epsilon = 1e-06

def project(inputs, blocks, mixing):
    tok_rows = inputs.shape[0]
    blocked = inputs.reshape(tok_rows * PHM, BLOCK)
    summed = jnp.zeros((tok_rows, PHM, BLOCK), jnp.float32)
    for term_index in range(PHM):
        product = jnp.dot(blocked, blocks[term_index], preferred_element_type=jnp.float32).reshape(tok_rows, PHM, BLOCK)
        summed = summed + jnp.einsum('tcg,cr->trg', product, mixing[term_index])
    return summed.reshape(tok_rows, D)

def reference(tokens, qkv_blocks, out_blocks, mix_factors, head_gain):
    nblk = SEQ // SPAN
    query_heads = project(tokens, qkv_blocks[0], mix_factors[0]).astype(jnp.bfloat16)
    key_heads = project(tokens, qkv_blocks[1], mix_factors[1]).astype(jnp.bfloat16)
    value_heads = project(tokens, qkv_blocks[2], mix_factors[2]).astype(jnp.bfloat16)
    query_f = query_heads.astype(jnp.float32).reshape(nblk, SPAN, HEADS, HEAD)
    key_f = key_heads.astype(jnp.float32).reshape(nblk, SPAN, HEADS, HEAD)
    value_f = value_heads.astype(jnp.float32).reshape(nblk, SPAN, HEADS, HEAD)
    states = jnp.einsum('nshd,nshe->nhde', key_f, value_f)
    running = jnp.cumsum(states, axis=0)
    prefix = jnp.concatenate([jnp.zeros_like(states[:1]), running[:-1]], axis=0)
    scores = jnp.einsum('nshd,nthd->nhst', query_f, key_f)
    causal = jnp.arange(SPAN)[:, None] >= jnp.arange(SPAN)[None, :]
    scores = jnp.where(causal[None, None], scores, 0.0).astype(jnp.bfloat16)
    within = jnp.einsum('nhst,nthe->nshe', scores.astype(jnp.float32), value_f)
    carried_out = jnp.einsum('nshd,nhde->nshe', query_f, prefix, precision=lax.Precision.HIGHEST)
    combined = within + carried_out
    mean_sq = lax.optimization_barrier(jnp.mean(combined * combined, axis=-1, keepdims=True))
    normed = combined * lax.rsqrt(mean_sq + epsilon) * head_gain.reshape(HEADS, HEAD)
    attn = normed.astype(jnp.bfloat16).reshape(SEQ, PHM, BLOCK)
    col_width = BLOCK // N_TP
    summed = jnp.zeros((SEQ, D), jnp.float32)
    for group_index in range(N_TP):
        columns = attn[:, :, group_index * col_width:(group_index + 1) * col_width].reshape(SEQ * PHM, col_width)
        partial_value = jnp.zeros((SEQ, PHM, BLOCK), jnp.float32)
        for term_index in range(PHM):
            rows_block = out_blocks[term_index, group_index * col_width:(group_index + 1) * col_width, :]
            product = jnp.dot(columns, rows_block, preferred_element_type=jnp.float32).reshape(SEQ, PHM, BLOCK)
            partial_value = partial_value + jnp.einsum('tch,cr->trh', product, mix_factors[3, term_index])
        rounded = lax.optimization_barrier(partial_value.reshape(SEQ, D).astype(jnp.bfloat16))
        summed = summed + rounded.astype(jnp.float32)
    return summed.astype(jnp.bfloat16)
```

```python
import functools

import jax
import jax.numpy as jnp
from jax import lax
from jax.experimental import pallas as pl
from jax.experimental.pallas import tpu as pltpu
from jax.sharding import PartitionSpec as P

PHM = 4
SPAN = 128
HEAD = 128
BLOCK = 1024


epsilon = 1e-06


def prefix_2(value, axis, combine, identity):
    devices, here = (lax.axis_size(axis), lax.axis_index(axis))
    everything = lax.all_gather(value.astype(jnp.bfloat16), axis)
    start = jnp.broadcast_to(jnp.asarray(identity, value.dtype), value.shape)

    def step(k, before):
        reached = k < here
        new = combine(before, everything[k].astype(value.dtype))
        return jnp.where(reached, new, before)

    return lax.fori_loop(0, devices, step, start)


def add_states(earlier, later):
    return earlier + later


def on_device(tokens, qkv_blocks, out_blocks, mix_factors, head_gain):
    whole = lax.all_gather(tokens, "tp", axis=1, tiled=True)
    tok_rows = whole.shape[0]
    col_width = qkv_blocks.shape[-1]
    local_heads = PHM * col_width // HEAD
    nblk = tok_rows // SPAN
    blocked = whole.reshape(tok_rows * PHM, BLOCK)

    def project(proj_idx):
        summed = jnp.zeros((tok_rows, PHM, col_width), jnp.float32)
        for term_index in range(PHM):
            product = jnp.dot(
                blocked, qkv_blocks[proj_idx, term_index], preferred_element_type=jnp.float32
            )
            product = product.reshape(tok_rows, PHM, col_width)
            summed = summed + jnp.einsum("tcg,cr->trg", product, mix_factors[proj_idx, term_index])
        return summed.astype(jnp.bfloat16).reshape(nblk, SPAN, local_heads, HEAD)

    query_heads = project(0)
    key_heads = project(1)
    value_heads = project(2)
    states = jnp.einsum(
        "nshd,nshe->nhde", key_heads, value_heads, preferred_element_type=jnp.float32
    )
    totals = jnp.sum(states, axis=0)
    earlier_sum = prefix_2(totals, "ctx", add_states, jnp.zeros_like(totals))
    running = jnp.cumsum(states, axis=0)
    prefix = jnp.concatenate([jnp.zeros_like(states[:1]), running[:-1]], axis=0) + earlier_sum[None]
    scores = jnp.einsum(
        "nshd,nthd->nhst", query_heads, key_heads, preferred_element_type=jnp.float32
    )
    causal = jnp.arange(SPAN)[:, None] >= jnp.arange(SPAN)[None, :]
    scores = jnp.where(causal[None, None], scores, 0.0).astype(jnp.bfloat16)
    within = jnp.einsum("nhst,nthe->nshe", scores, value_heads, preferred_element_type=jnp.float32)
    carried_out = jnp.einsum(
        "nshd,nhde->nshe", query_heads.astype(jnp.float32), prefix, precision=lax.Precision.HIGHEST
    )
    combined = within + carried_out
    mean_sq = jnp.mean(combined * combined, axis=-1, keepdims=True)
    normed = combined * lax.rsqrt(mean_sq + epsilon) * head_gain.reshape(local_heads, HEAD)
    attn = normed.astype(jnp.bfloat16).reshape(tok_rows * PHM, col_width)
    partial_value = jnp.zeros((tok_rows, PHM, BLOCK), jnp.float32)
    for term_index in range(PHM):
        product = jnp.dot(attn, out_blocks[term_index], preferred_element_type=jnp.float32).reshape(
            tok_rows, PHM, BLOCK
        )
        partial_value = partial_value + jnp.einsum(
            "tch,cr->trh", product, mix_factors[3, term_index]
        )
    reduced = lax.psum_scatter(
        partial_value.reshape(tok_rows, PHM * BLOCK).astype(jnp.bfloat16),
        "tp",
        scatter_dimension=1,
        tiled=True,
    )
    return reduced


MESH = pl.DeviceIdType.MESH
CHUNKS = 4
TILE = 256
bf16 = jnp.bfloat16
f32 = jnp.float32


def layer_kernel(
    depth,
    tokens,
    qkv_blocks,
    out_blocks,
    gain,
    mix,
    out,
    gathered,
    blocks,
    weights,
    acc,
    qkv,
    mixed,
    out_weights,
    for_sibling,
    for_partner,
    direct,
    from_forward,
    from_sibling,
    from_partner,
    staged,
    total,
    total_half,
    y_recv,
    z_recv,
    z_send,
    m_send,
    m_recv,
    prefix,
    local_sem,
    block_sem,
    sib_sem,
    par_sem,
    fwd_sem,
    y_sem,
    z_sem,
    m_sem,
    a_sem,
    b_sem,
    c_sem,
    out_sem,
):
    ctx, tp = lax.axis_index("ctx"), lax.axis_index("tp")
    z, y = ctx // 2, ctx % 2
    chip, core = tp // 2, tp % 2
    sibling = chip * 2 + 1 - core
    partner = (1 - chip) * 2 + core
    diagonal = (1 - chip) * 2 + 1 - core
    y_peer = z * 2 + 1 - y
    rows = tokens.shape[0]
    step = rows // CHUNKS
    heads = 8
    half = heads // 2

    def remote(src, dst, sems, k, where):
        return pltpu.make_async_remote_copy(
            src_ref=src,
            dst_ref=dst,
            send_sem=sems.at[0, k],
            recv_sem=sems.at[1, k],
            device_id=where,
            device_id_type=MESH,
        )

    def chunk(j):
        return pl.ds(pl.multiple_of(j * step, step), step)

    own_copy = pltpu.make_async_copy(tokens, gathered.at[0], local_sem.at[0])
    out_copy = pltpu.make_async_copy(out_blocks, out_weights, local_sem.at[1])
    block_copies = [
        pltpu.make_async_copy(qkv_blocks.at[p], blocks.at[p], block_sem.at[p]) for p in range(3)
    ]
    for c in block_copies:
        c.start()
    own_copy.start()
    out_copy.start()

    barrier = pltpu.get_barrier_semaphore()
    for where in ((ctx, sibling), (ctx, partner), (y_peer, tp)):
        pl.semaphore_signal(barrier, inc=1, device_id=where, device_id_type=MESH)

    @pl.when(z > 0)
    def _():
        pl.semaphore_signal(barrier, inc=1, device_id=(ctx - 2, tp), device_id_type=MESH)

    @pl.when(z < depth - 1)
    def _():
        pl.semaphore_signal(barrier, inc=1, device_id=(ctx + 2, tp), device_id_type=MESH)

    pl.semaphore_wait(barrier, 3 + jnp.minimum(z, 1) + jnp.minimum(depth - 1 - z, 1))

    def to_partner(j):
        return remote(
            tokens.at[chunk(j)], gathered.at[2, chunk(j)], par_sem, j, (ctx, partner)
        )

    def forward(j):
        return remote(
            gathered.at[2, chunk(j)], gathered.at[3, chunk(j)], fwd_sem, j, (ctx, sibling)
        )

    for j in range(CHUNKS):
        to_partner(j).start()
    to_sibling = remote(tokens, gathered.at[1], sib_sem, 0, (ctx, sibling))
    to_sibling.start()

    lines = 32

    for p in range(3):
        block_copies[p].wait()

        def combine(k, carry, p=p):
            at = pl.ds(pl.multiple_of(k * lines, lines), lines)
            terms = [blocks[p, i, at, :].astype(f32) for i in range(PHM)]
            for c in range(PHM):
                for r in range(PHM):
                    w = terms[0] * mix[p, 0, c, r]
                    for i in range(1, PHM):
                        w = w + terms[i] * mix[p, i, c, r]
                    lo = p * BLOCK + r * TILE
                    weights[c, at, lo : lo + TILE] = w.astype(bf16)
            return carry

        lax.fori_loop(0, BLOCK // lines, combine, 0)

    def tile(t):
        return pl.ds(pl.multiple_of(t * TILE, TILE), TILE)

    tiles = 3 * BLOCK // TILE
    own_copy.wait()

    def project_own(t, carry):
        acc[:, tile(t)] = jnp.dot(gathered[0], weights[tp, :, tile(t)], preferred_element_type=f32)
        return carry

    lax.fori_loop(0, tiles, project_own, 0)
    to_sibling.wait()

    def project_sibling(t, carry):
        acc[:, tile(t)] += jnp.dot(
            gathered[1], weights[sibling, :, tile(t)], preferred_element_type=f32
        )
        return carry

    lax.fori_loop(0, tiles, project_sibling, 0)

    def head(p, h):
        return pl.ds(pl.multiple_of(p * BLOCK + h * HEAD, HEAD), HEAD)

    total[...] = jnp.zeros_like(total)

    def finish_chunk(j, carry):
        to_partner(j).wait()
        forward(j).start()
        forward(j).wait()

        def one(t, inner):
            got = acc[chunk(j), tile(t)]
            got += jnp.dot(
                gathered[2, chunk(j), :], weights[partner, :, tile(t)], preferred_element_type=f32
            )
            got += jnp.dot(
                gathered[3, chunk(j), :], weights[diagonal, :, tile(t)], preferred_element_type=f32
            )
            qkv[chunk(j), tile(t)] = got.astype(bf16)
            return inner

        lax.fori_loop(0, tiles, one, 0)
        for h in range(heads):
            total[h] += lax.dot_general(
                qkv[chunk(j), head(1, h)],
                qkv[chunk(j), head(2, h)],
                (((0,), (0,)), ((), ())),
                preferred_element_type=f32,
            )
        return carry

    lax.fori_loop(0, CHUNKS, finish_chunk, 0)

    mine, other = y * half, (1 - y) * half
    for h in range(half):
        total_half[h] = total[other + h].astype(bf16)
    y_copy = remote(total_half, y_recv, y_sem, 0, (y_peer, tp))
    y_copy.start()

    def within(h, carry):
        for part in range(2):
            first, last = part * rows // 2, (part + 1) * rows // 2
            scores = lax.dot_general(
                qkv[first:last, head(0, h)],
                qkv[0:last, head(1, h)],
                (((1,), (1,)), ((), ())),
                preferred_element_type=f32,
            )
            t_pos = lax.broadcasted_iota(jnp.int32, scores.shape, 0) + first
            s_pos = lax.broadcasted_iota(jnp.int32, scores.shape, 1)
            scores = jnp.where(t_pos >= s_pos, scores, 0.0).astype(bf16)
            acc[first:last, head(0, h)] = jnp.dot(
                scores, qkv[0:last, head(2, h)], preferred_element_type=f32
            )
        return carry

    early = heads - 2 * (depth - 1 - z)
    lax.fori_loop(0, early, within, 0)
    y_copy.wait()

    def down(h):
        return remote(z_send.at[h], z_recv.at[h], z_sem, h, (ctx + 2, tp))

    def up(h):
        return remote(z_send.at[h], z_recv.at[h], z_sem, h, (ctx - 2, tp))

    def share(h):
        return remote(m_send.at[h], m_recv.at[h], m_sem, h, (y_peer, tp))

    @pl.when(z == 0)
    def _():
        z_recv[...] = jnp.zeros_like(z_recv)

    for h in range(half):

        @pl.when(z > 0)
        def _():
            up(h).wait_recv()

        before = z_recv[h].astype(f32)
        own = total[mine + h]
        peer = y_recv[h].astype(f32)

        @pl.when(z < depth - 1)
        def _():
            z_send[h] = (before + own + peer).astype(bf16)
            down(h).start()

        m_send[h] = (before + jnp.where(y == 0, own, 0.0)).astype(bf16)
        share(h).start()
        prefix[mine + h] = (before + jnp.where(y == 0, 0.0, peer)).astype(bf16)

    lax.fori_loop(early, heads, within, 0)
    out_copy.wait()

    for h in range(half):
        share(h).wait()
        prefix[other + h] = m_recv[h]

    def to_forwarder(j):
        return remote(
            for_sibling.at[chunk(j)], from_forward.at[chunk(j)], a_sem, j, (ctx, sibling)
        )

    def across(j):
        return remote(
            for_partner.at[chunk(j)], from_partner.at[chunk(j)], b_sem, j, (ctx, partner)
        )

    def beside(j):
        return remote(direct.at[chunk(j)], from_sibling.at[chunk(j)], c_sem, j, (ctx, sibling))

    def group_term(j, r, store):
        def one(t, carry):
            store(
                tile(t),
                jnp.dot(
                    mixed[r, chunk(j), :], out_weights[:, tile(t)], preferred_element_type=f32
                ),
            )
            return carry

        lax.fori_loop(0, BLOCK // TILE, one, 0)

    def attend(j, carry):
        for h in range(heads):
            combined = acc[chunk(j), head(0, h)] + jnp.dot(
                qkv[chunk(j), head(0, h)], prefix[h], preferred_element_type=f32
            )
            mean_sq = jnp.mean(combined * combined, axis=-1, keepdims=True)
            lo = (h % 2) * HEAD
            g = gain[h // 2 : h // 2 + 1, lo : lo + HEAD]
            acc[chunk(j), head(1, h)] = combined * lax.rsqrt(mean_sq + epsilon) * g

        def mix_rows(k, inner):
            at = pl.ds(pl.multiple_of(j * step + k * lines, lines), lines)
            parts = [acc[at, BLOCK + c * TILE : BLOCK + (c + 1) * TILE] for c in range(PHM)]
            for r in range(PHM):
                for i in range(PHM):
                    v = parts[0] * mix[3, i, 0, r]
                    for c in range(1, PHM):
                        v = v + parts[c] * mix[3, i, c, r]
                    mixed[r, at, i * TILE : (i + 1) * TILE] = v.astype(bf16)
            return inner

        lax.fori_loop(0, step // lines, mix_rows, 0)

        def store_forwarded(cols, value):
            for_sibling[chunk(j), cols] = value.astype(bf16)

        group_term(j, diagonal, store_forwarded)
        to_forwarder(j).start()

        def store_partner_f32(t, inner):
            at = pl.ds(pl.multiple_of(2 * BLOCK + t * TILE, TILE), TILE)
            acc[chunk(j), at] = jnp.dot(
                mixed[partner, chunk(j), :], out_weights[:, tile(t)], preferred_element_type=f32
            )
            return inner

        lax.fori_loop(0, BLOCK // TILE, store_partner_f32, 0)
        to_forwarder(j).wait()
        for_partner[chunk(j), :] = (
            acc[chunk(j), 2 * BLOCK :] + from_forward[chunk(j), :].astype(f32)
        ).astype(bf16)
        across(j).start()
        return carry

    lax.fori_loop(0, CHUNKS, attend, 0)

    def stay(j, carry):
        def store_direct(cols, value):
            direct[chunk(j), cols] = value.astype(bf16)

        group_term(j, sibling, store_direct)
        beside(j).start()

        def store_own(cols, value):
            acc[chunk(j), cols] = value

        group_term(j, tp, store_own)
        return carry

    lax.fori_loop(0, CHUNKS, stay, 0)

    def put(j):
        return pltpu.make_async_copy(staged.at[chunk(j)], out.at[chunk(j)], out_sem.at[j])

    def finish(j, carry):
        beside(j).wait()
        across(j).wait()
        staged[chunk(j), :] = (
            acc[chunk(j), :BLOCK]
            + from_sibling[chunk(j), :].astype(f32)
            + from_partner[chunk(j), :].astype(f32)
        ).astype(bf16)
        put(j).start()
        return carry

    lax.fori_loop(0, CHUNKS, finish, 0)
    for j in range(CHUNKS):
        put(j).wait()

    @pl.when(z < depth - 1)
    def _():
        for h in range(half):
            down(h).wait_send()


def in_one_kernel(depth, tokens, qkv_blocks, out_blocks, mix_factors, head_gain):
    rows, width = tokens.shape
    state = (HEAD, HEAD)
    vmem = pltpu.VMEM
    return pl.pallas_call(
        functools.partial(layer_kernel, depth),
        out_shape=jax.ShapeDtypeStruct((rows, width), bf16),
        in_specs=[
            pl.BlockSpec(memory_space=pl.ANY),
            pl.BlockSpec(memory_space=pl.ANY),
            pl.BlockSpec(memory_space=pl.ANY),
            pl.BlockSpec(memory_space=pltpu.VMEM),
            pl.BlockSpec(memory_space=pltpu.SMEM),
        ],
        out_specs=pl.BlockSpec(memory_space=pl.ANY),
        scratch_shapes=[
            vmem((4, rows, BLOCK), bf16),
            vmem(qkv_blocks.shape, bf16),
            vmem((PHM, BLOCK, 3 * BLOCK), bf16),
            vmem((rows, 3 * BLOCK), f32),
            vmem((rows, 3 * BLOCK), bf16),
            vmem((PHM, rows, BLOCK), bf16),
            vmem((BLOCK, BLOCK), bf16),
            vmem((rows, BLOCK), bf16),
            vmem((rows, BLOCK), bf16),
            vmem((rows, BLOCK), bf16),
            vmem((rows, BLOCK), bf16),
            vmem((rows, BLOCK), bf16),
            vmem((rows, BLOCK), bf16),
            vmem((rows, BLOCK), bf16),
            vmem((8,) + state, f32),
            vmem((4,) + state, bf16),
            vmem((4,) + state, bf16),
            vmem((4,) + state, bf16),
            vmem((4,) + state, bf16),
            vmem((4,) + state, bf16),
            vmem((4,) + state, bf16),
            vmem((8,) + state, bf16),
            pltpu.SemaphoreType.DMA((2,)),
            pltpu.SemaphoreType.DMA((3,)),
            pltpu.SemaphoreType.DMA((2, 1)),
            pltpu.SemaphoreType.DMA((2, CHUNKS)),
            pltpu.SemaphoreType.DMA((2, CHUNKS)),
            pltpu.SemaphoreType.DMA((2, 1)),
            pltpu.SemaphoreType.DMA((2, 4)),
            pltpu.SemaphoreType.DMA((2, 4)),
            pltpu.SemaphoreType.DMA((2, CHUNKS)),
            pltpu.SemaphoreType.DMA((2, CHUNKS)),
            pltpu.SemaphoreType.DMA((2, CHUNKS)),
            pltpu.SemaphoreType.DMA((CHUNKS,)),
        ],
        compiler_params=pltpu.CompilerParams(
            collective_id=0, has_side_effects=True, vmem_limit_bytes=63 * 1024 * 1024
        ),
    )(tokens, qkv_blocks, out_blocks.reshape(BLOCK, BLOCK), head_gain, mix_factors)


def solution(mesh):
    placed = (P("ctx", "tp"), P(None, None, None, "tp"), P(None, "tp", None), P(), P(None, "tp"))
    run = on_device
    if mesh.shape["tp"] == PHM and mesh.shape["ctx"] == 8:
        run = functools.partial(in_one_kernel, mesh.shape["ctx"] // 2)
    return jax.shard_map(
        run, mesh=mesh, in_specs=placed, out_specs=P("ctx", "tp"), check_vma=False
    )
```
